32 devices in a mesh: gx: 8 (over z, x), gy: 4 (over y, core).
Axes of the slice: x: 2, y: 2, z: 4, core: 2. Of those that a mesh axis runs over, the one named last changes fastest.
Arguments:
- velocity: float32 [3, 64, 64, 128], P(None, 'gx', 'gy'), may hold values from -6 to 6
- stress: float32 [6, 64, 64, 128], P(None, 'gx', 'gy'), may hold values from -6 to 6
- lame_first: float32 [64, 64, 128], P('gx', 'gy'), may hold values from 0.5 to 1.5
- shear_modulus: float32 [64, 64, 128], P('gx', 'gy'), may hold values from 0.3 to 1
- buoyancy: float32 [64, 64, 128], P('gx', 'gy'), may hold values from 0.5 to 1
- forward_strain: bfloat16 [12, 64, 64, 128], P(None, 'gx', 'gy'), may hold values from -6 to 6
- lame_accum: float32 [64, 64, 128], P('gx', 'gy'), may hold values from -6 to 6
- shear_accum: float32 [64, 64, 128], P('gx', 'gy'), may hold values from -6 to 6
- residuals: bfloat16 [1024, 4096], P(('gx', 'gy')), may hold values from -24 to 24
- station_cell: int32 [1024], P(('gx', 'gy')), may hold values from 0 to 127
- station_pairs: int32 [4096, 2], replicated, may hold values from 0 to 1023, as said below
Outputs:
- new_velocity: float32 [3, 64, 64, 128], P(None, 'gx', 'gy')
- new_stress: float32 [6, 64, 64, 128], P(None, 'gx', 'gy')
- lame_kernel: float32 [64, 64, 128], P('gx', 'gy')
- shear_kernel: float32 [64, 64, 128], P('gx', 'gy')
- adjoint_source: float32 [1024, 4096], P(('gx', 'gy'))
The draws below stay inside these ranges and needn't reach their ends.
Inputs may be any that keep to these rules, and one draw needn't show every extreme that they name: station_cell[s] numbers the surface cell x * 16 + y of station s within the block of the device that holds station s. `station_pairs`: stations s * 32 to (s + 1) * 32 - 1 are held by device s of gx+gy. The first station of pair p is held by device p // 128. Among the 128 pairs of one device, at most 8 have a second station held by any one device; some may have none. Some device's stations are the second station of exactly 8 pairs of every device.
All inputs are finite; a program needn't handle non-finite values.
Results may differ from the reference program's by a relative error of at most 0.0017.
Values may be sent and summed in bfloat16 or wider, within the bound.
A program may use at most 64 MiB of HBM per device.

```python
import math
import jax
import jax.numpy as jnp
from jax import lax

CX = 8
CY = 16
NSAMP = 4096
STEPS = 2
STA_DEV = 32
P_DEV = 128
NX = 64
NY = 64
NZ = 128
STATIONS = 1024
PAIRS = 4096
CAP = 8
SLOTS = 256
N_GY = 4


def draw_residuals(key, part):
    common = jnp.clip(jax.random.normal(jax.random.fold_in(key, 21), (NSAMP,), jnp.float32), -4.0, 4.0)
    mixing = jax.random.uniform(jax.random.fold_in(key, 22), (STATIONS, 1), jnp.float32, 0.0, 1.5)
    own_part = jnp.clip(jax.random.normal(jax.random.fold_in(key, 23), (STATIONS, NSAMP), jnp.float32), -4.0, 4.0)
    station_gain = jnp.exp(jax.random.uniform(jax.random.fold_in(key, 24), (STATIONS, 1), jnp.float32, math.log(0.3), math.log(3.0)))
    return (station_gain * (0.7 * mixing * common[None, :] + 0.7 * own_part)).astype(jnp.bfloat16)


def draw_station_pairs(key, part):
    devices = PAIRS // P_DEV
    owner_level = jax.random.randint(jax.random.fold_in(key, 11), (devices,), 0, 3)
    hottest = jax.random.randint(jax.random.fold_in(key, 12), (), 0, devices)
    slot_owner = jnp.arange(SLOTS) // CAP

    def one_device(device_number):
        device_key = jax.random.fold_in(key, 1000 + device_number)
        ranking = jax.random.permutation(jax.random.fold_in(device_key, 1), SLOTS)
        slot_score = jnp.where(slot_owner == hottest, ranking - SLOTS, owner_level[slot_owner] * SLOTS + ranking)
        chosen = jnp.argsort(slot_score, stable=True)[:P_DEV]
        owners = chosen // CAP
        second_station = owners * STA_DEV + jax.random.randint(jax.random.fold_in(device_key, 2), (P_DEV,), 0, STA_DEV)
        first_station = device_number * STA_DEV + jax.random.randint(jax.random.fold_in(device_key, 3), (P_DEV,), 0, STA_DEV)
        return jnp.stack([first_station, second_station], axis=1)
    return jax.vmap(one_device)(jnp.arange(devices)).reshape(PAIRS, 2).astype(jnp.int32)


def plant(result, own_key, least, high):
    longest = result.shape.index(max(result.shape))
    spots = []
    for shift in (0, 1):
        where = [jax.random.randint(jax.random.fold_in(own_key, axis), (), 0, length) for axis, length in enumerate(result.shape)]
        where[longest] = (where[longest] + shift) % result.shape[longest]
        spots.append(tuple(where))
    return result.at[spots[0]].set(least).at[spots[1]].set(high)


def levels(rng, shape, shards, low, top_value):
    def one(dim, shards_of):
        draws = jax.random.uniform(jax.random.fold_in(jax.random.fold_in(rng, 6), dim), (shards_of,), jnp.float32, low / len(shards), top_value / len(shards))
        return jnp.repeat(jnp.exp(draws), shape[dim] // shards_of).reshape((-1,) + (1,) * (len(shape) - dim - 1))

    factor_of = one(*shards[0])
    for cut in shards[1:]:
        factor_of = factor_of * one(*cut)
    return factor_of


def noise(own_key, shape, scale, limit, shards=(), kind=jnp.bfloat16):
    result = scale * jax.random.normal(own_key, shape, jnp.float32)
    if shards:
        result = result * levels(own_key, shape, shards, -0.22, 0.18)
    return jnp.clip(result, -limit, limit).astype(kind)


def setup_inputs(seed: int = 0) -> dict:
    keys = jax.random.split(jax.random.key(seed), 12)
    return {
        "velocity": noise(keys[0], (3, NX, NY, NZ), 1.0, 6.0, ((1, 8), (2, 4)), jnp.float32),
        "stress": noise(keys[1], (6, NX, NY, NZ), 1.0, 6.0, ((1, 8), (2, 4)), jnp.float32),
        "lame_first": jnp.clip(jnp.exp(math.log(1.5) - 1.0986123 * jax.random.uniform(keys[2], (NX, NY, NZ), jnp.float32) ** levels(keys[2], (NX, NY, NZ), ((0, 8), (1, 4)), -0.2, 0.2)), 0.5, 1.5),
        "shear_modulus": jnp.clip(jnp.exp(math.log(1.0) - 1.2039728 * jax.random.uniform(keys[3], (NX, NY, NZ), jnp.float32) ** levels(keys[3], (NX, NY, NZ), ((0, 8), (1, 4)), -0.2, 0.2)), 0.3, 1.0),
        "buoyancy": jnp.clip(jnp.exp(math.log(1.0) - 0.6931472 * jax.random.uniform(keys[4], (NX, NY, NZ), jnp.float32) ** levels(keys[4], (NX, NY, NZ), ((0, 8), (1, 4)), -0.2, 0.2)), 0.5, 1.0),
        "forward_strain": noise(keys[5], (STEPS * 6, NX, NY, NZ), 1.0, 6.0, ((1, 8), (2, 4))),
        "lame_accum": noise(keys[6], (NX, NY, NZ), 1.0, 6.0, ((0, 8), (1, 4)), jnp.float32),
        "shear_accum": noise(keys[7], (NX, NY, NZ), 1.0, 6.0, ((0, 8), (1, 4)), jnp.float32),
        "residuals": draw_residuals(jax.random.fold_in(keys[11], 71), 0),
        "station_cell": plant(jax.random.randint(keys[9], (STATIONS,), 0, CX * CY), jax.random.fold_in(keys[9], 1), 0, (CX * CY) - 1).astype(jnp.int32),
        "station_pairs": draw_station_pairs(jax.random.fold_in(keys[11], 71), 0),
    }


near_weight = 9.0 / 8.0
far_weight = -1.0 / 24.0
time_step = 0.25
epsilon = 1e-06

def shifted(padded, start, length, axis):
    return lax.slice_in_dim(padded, start, start + length, axis=axis)

def backward_diff(padded, length, axis):
    return near_weight * (shifted(padded, 2, length, axis) - shifted(padded, 1, length, axis)) + far_weight * (shifted(padded, 3, length, axis) - shifted(padded, 0, length, axis))

def forward_diff(padded, length, axis):
    return near_weight * (shifted(padded, 3, length, axis) - shifted(padded, 2, length, axis)) + far_weight * (shifted(padded, 4, length, axis) - shifted(padded, 1, length, axis))

def padded_three(field):
    return (jnp.pad(field, ((0, 0), (2, 2), (0, 0), (0, 0))), jnp.pad(field, ((0, 0), (0, 0), (2, 2), (0, 0))), jnp.pad(field, ((0, 0), (0, 0), (0, 0), (2, 2))))

def advance(velocity, stress, lame_first, shear_modulus, buoyancy, strain_now, surface, lame_kernel, shear_kernel):
    cells_first = velocity.shape[1]
    cells_second = velocity.shape[2]
    cells_third = velocity.shape[3]
    stress_first, stress_second, stress_third = padded_three(stress)
    force_first = forward_diff(stress_first[0], cells_first, 0) + backward_diff(stress_second[3], cells_second, 1) + backward_diff(stress_third[4], cells_third, 2)
    force_second = backward_diff(stress_first[3], cells_first, 0) + forward_diff(stress_second[1], cells_second, 1) + backward_diff(stress_third[5], cells_third, 2)
    force_third = backward_diff(stress_first[4], cells_first, 0) + backward_diff(stress_second[5], cells_second, 1) + forward_diff(stress_third[2], cells_third, 2)
    force_third = force_third.at[:, :, 0].add(surface)
    moved = velocity + time_step * buoyancy[None] * jnp.stack([force_first, force_second, force_third])
    motion_first, motion_second, motion_third = padded_three(moved)
    rate_first = backward_diff(motion_first[0], cells_first, 0)
    rate_second = backward_diff(motion_second[1], cells_second, 1)
    rate_third = backward_diff(motion_third[2], cells_third, 2)
    shear_one = forward_diff(motion_second[0], cells_second, 1) + forward_diff(motion_first[1], cells_first, 0)
    shear_two = forward_diff(motion_third[0], cells_third, 2) + forward_diff(motion_first[2], cells_first, 0)
    shear_three = forward_diff(motion_third[1], cells_third, 2) + forward_diff(motion_second[2], cells_second, 1)
    dilation = rate_first + rate_second + rate_third
    grown = stress + time_step * jnp.stack([lame_first * dilation + 2.0 * shear_modulus * rate_first, lame_first * dilation + 2.0 * shear_modulus * rate_second, lame_first * dilation + 2.0 * shear_modulus * rate_third, shear_modulus * shear_one, shear_modulus * shear_two, shear_modulus * shear_three])
    strain_vals = strain_now.astype(jnp.float32)
    lame_kernel = lame_kernel + time_step * (strain_vals[0] + strain_vals[1] + strain_vals[2]) * dilation
    shear_kernel = shear_kernel + 2.0 * time_step * (strain_vals[0] * rate_first + strain_vals[1] * rate_second + strain_vals[2] * rate_third + strain_vals[3] * shear_one + strain_vals[4] * shear_two + strain_vals[5] * shear_three)
    return (moved, grown, lame_kernel, shear_kernel)

def reference(velocity, stress, lame_first, shear_modulus, buoyancy, forward_strain, lame_accum, shear_accum, residuals, station_cell, station_pairs):
    values = residuals.astype(jnp.float32)
    normed = values / jnp.sqrt(lax.optimization_barrier(jnp.mean(values * values, axis=1, keepdims=True)) + epsilon)
    blocks = station_pairs.reshape(PAIRS // P_DEV, P_DEV, 2)

    def add_block(total, block):
        first_vals = normed[block[:, 0]]
        second_vals = normed[block[:, 1]]
        corr = lax.optimization_barrier(jnp.mean(first_vals * second_vals, axis=1, keepdims=True))
        toward_first = lax.optimization_barrier((second_vals - corr * first_vals).astype(jnp.bfloat16)).astype(jnp.float32)
        toward_second = lax.optimization_barrier((first_vals - corr * second_vals).astype(jnp.bfloat16)).astype(jnp.float32)
        total = total.at[block[:, 0]].add(toward_first)
        total = total.at[block[:, 1]].add(toward_second)
        return (total, None)
    adjoint, ignored = lax.scan(add_block, jnp.zeros((STATIONS, NSAMP), jnp.float32), blocks)
    holder = (jnp.arange(STATIONS) // STA_DEV).astype(jnp.int32)
    across_pos = (holder // N_GY * CX + station_cell // CY).astype(jnp.int32)
    along_pos = (holder % N_GY * CY + station_cell % CY).astype(jnp.int32)
    for window_step in range(STEPS):
        surface = jnp.zeros((NX, NY), jnp.float32).at[across_pos, along_pos].add(adjoint[:, NSAMP - 1 - window_step])
        strain_now = forward_strain[6 * window_step:6 * window_step + 6]
        velocity, stress, lame_accum, shear_accum = advance(velocity, stress, lame_first, shear_modulus, buoyancy, strain_now, surface, lame_accum, shear_accum)
    return (velocity, stress, lame_accum, shear_accum, adjoint)
```

```python
import jax
import jax.numpy as jnp
from jax import lax
from jax.sharding import PartitionSpec as P

near_weight = 9.0 / 8.0
far_weight = -1.0 / 24.0
time_step = 0.25
epsilon = 1e-06


def halos(block, axis, dim, width=2):
    count = lax.axis_size(axis)
    forward = [(i, i + 1) for i in range(count - 1)]
    backward = [(target, source) for source, target in forward]
    low = lax.ppermute(
        lax.slice_in_dim(block, block.shape[dim] - width, None, axis=dim), axis, forward
    )
    high = lax.ppermute(lax.slice_in_dim(block, 0, width, axis=dim), axis, backward)
    return jnp.concatenate([low, block, high], axis=dim)


def shifted(padded, start, length, axis):
    return lax.slice_in_dim(padded, start, start + length, axis=axis)


def backward_diff(padded, length, axis):
    return near_weight * (
        shifted(padded, 2, length, axis) - shifted(padded, 1, length, axis)
    ) + far_weight * (shifted(padded, 3, length, axis) - shifted(padded, 0, length, axis))


def forward_diff(padded, length, axis):
    return near_weight * (
        shifted(padded, 3, length, axis) - shifted(padded, 2, length, axis)
    ) + far_weight * (shifted(padded, 4, length, axis) - shifted(padded, 1, length, axis))


def split_halves(value):
    top = lax.reduce_precision(value, 8, 7)
    return top.astype(jnp.bfloat16), (value - top).astype(jnp.bfloat16)


def partner_sums(scaled, station_pairs, devices):
    stations = scaled.shape[0]
    pairs = station_pairs.shape[0]
    if stations > 1024:
        first, second = station_pairs[:, 0], station_pairs[:, 1]
        total = jnp.zeros_like(scaled).at[first].add(scaled[second])
        return total.at[second].add(scaled[first])
    held = stations // devices
    blocks = station_pairs.reshape(devices, pairs // devices, 2)
    offset = jnp.arange(devices)[:, None] * held
    first_hot = ((blocks[:, :, 0] - offset)[:, :, None] == jnp.arange(held)).astype(jnp.bfloat16)
    second_hot = (blocks[:, :, 1][:, :, None] == jnp.arange(stations)).astype(jnp.bfloat16)
    counts = (
        jnp.einsum("bpj,bpt->bjt", first_hot, second_hot, preferred_element_type=jnp.float32)
        .astype(jnp.bfloat16)
        .reshape(stations, stations)
    )
    both = jnp.concatenate(split_halves(scaled), axis=1)
    width = scaled.shape[1]
    total = lax.dot_general(
        counts, both, (((1,), (0,)), ((), ())), preferred_element_type=jnp.float32
    ) + lax.dot_general(
        counts, both, (((0,), (0,)), ((), ())), preferred_element_type=jnp.float32
    )
    return total[:, :width] + total[:, width:]


def adjoint_rows(residuals, station_pairs):
    axes = ("gx", "gy")
    held, samples = residuals.shape
    devices = lax.axis_size(axes)
    chunk = samples // devices
    values = residuals.astype(jnp.float32)
    inverse = 1.0 / jnp.sqrt(jnp.mean(values * values, axis=1, keepdims=True) + epsilon)
    inverse_top, inverse_rest = split_halves(inverse.reshape(1, held))
    scales = jnp.concatenate([inverse_top, inverse_rest], axis=0)
    scales = jnp.pad(scales, ((0, 14), (0, chunk - held)))
    payload = jnp.concatenate(
        [
            residuals.reshape(held, devices, chunk).transpose(1, 0, 2),
            jnp.broadcast_to(scales[None], (devices, 16, chunk)),
        ],
        axis=1,
    )
    arrived = lax.all_to_all(payload, axes, split_axis=0, concat_axis=0, tiled=True)
    arrived_scales = arrived[:, held, :held].astype(jnp.float32) + arrived[
        :, held + 1, :held
    ].astype(jnp.float32)
    scaled = (arrived[:, :held].astype(jnp.float32) * arrived_scales[:, :, None]).reshape(
        devices * held, chunk
    )
    sums = partner_sums(scaled, station_pairs, devices).reshape(devices, held, chunk)
    back = lax.all_to_all(sums, axes, split_axis=0, concat_axis=0, tiled=True)
    back = back.transpose(1, 0, 2).reshape(held, samples)
    normed = values * inverse
    corr_sum = jnp.mean(normed * back, axis=1, keepdims=True)
    return back - corr_sum * normed


def stress_sides(stress):
    first = halos(jnp.stack([stress[0], stress[3], stress[4]]), "gx", 1)
    second = halos(jnp.stack([stress[1], stress[3], stress[5]]), "gy", 2)
    return (first, second)


def motion_sides(moved):
    return (halos(moved, "gx", 1), halos(moved, "gy", 2))


def advance(
    velocity,
    stress,
    lame_first,
    shear_modulus,
    buoyancy,
    strain_now,
    surface,
    lame_kernel,
    shear_kernel,
):
    cells_first = velocity.shape[1]
    cells_second = velocity.shape[2]
    cells_third = velocity.shape[3]
    across_stress, along_stress = stress_sides(stress)
    stress_third = jnp.pad(stress, ((0, 0), (0, 0), (0, 0), (2, 2)))
    force_first = (
        forward_diff(across_stress[0], cells_first, 0)
        + backward_diff(along_stress[1], cells_second, 1)
        + backward_diff(stress_third[4], cells_third, 2)
    )
    force_second = (
        backward_diff(across_stress[1], cells_first, 0)
        + forward_diff(along_stress[0], cells_second, 1)
        + backward_diff(stress_third[5], cells_third, 2)
    )
    force_third = (
        backward_diff(across_stress[2], cells_first, 0)
        + backward_diff(along_stress[2], cells_second, 1)
        + forward_diff(stress_third[2], cells_third, 2)
    )
    force_third = force_third.at[:, :, 0].add(surface)
    moved = velocity + time_step * buoyancy[None] * jnp.stack(
        [force_first, force_second, force_third]
    )
    motion_first, motion_second = motion_sides(moved)
    motion_third = jnp.pad(moved, ((0, 0), (0, 0), (0, 0), (2, 2)))
    rate_first = backward_diff(motion_first[0], cells_first, 0)
    rate_second = backward_diff(motion_second[1], cells_second, 1)
    rate_third = backward_diff(motion_third[2], cells_third, 2)
    shear_one = forward_diff(motion_second[0], cells_second, 1) + forward_diff(
        motion_first[1], cells_first, 0
    )
    shear_two = forward_diff(motion_third[0], cells_third, 2) + forward_diff(
        motion_first[2], cells_first, 0
    )
    shear_three = forward_diff(motion_third[1], cells_third, 2) + forward_diff(
        motion_second[2], cells_second, 1
    )
    dilation = rate_first + rate_second + rate_third
    grown = stress + time_step * jnp.stack(
        [
            lame_first * dilation + 2.0 * shear_modulus * rate_first,
            lame_first * dilation + 2.0 * shear_modulus * rate_second,
            lame_first * dilation + 2.0 * shear_modulus * rate_third,
            shear_modulus * shear_one,
            shear_modulus * shear_two,
            shear_modulus * shear_three,
        ]
    )
    strain_vals = strain_now.astype(jnp.float32)
    lame_kernel = (
        lame_kernel + time_step * (strain_vals[0] + strain_vals[1] + strain_vals[2]) * dilation
    )
    shear_kernel = shear_kernel + 2.0 * time_step * (
        strain_vals[0] * rate_first
        + strain_vals[1] * rate_second
        + strain_vals[2] * rate_third
        + strain_vals[3] * shear_one
        + strain_vals[4] * shear_two
        + strain_vals[5] * shear_three
    )
    return (moved, grown, lame_kernel, shear_kernel)


def shards(
    velocity,
    stress,
    lame_first,
    shear_modulus,
    buoyancy,
    forward_strain,
    lame_accum,
    shear_accum,
    residuals,
    station_cell,
    station_pairs,
):
    samples = residuals.shape[1]
    adjoint = adjoint_rows(residuals, station_pairs)
    cells_first = velocity.shape[1]
    cells_second = velocity.shape[2]
    step_count = forward_strain.shape[0] // 6
    cells_hit = (station_cell[:, None] == jnp.arange(cells_first * cells_second)[None, :]).astype(
        jnp.float32
    )
    surfaces = jnp.stack(
        [
            jnp.sum(cells_hit * adjoint[:, samples - 1 - window_step][:, None], axis=0).reshape(
                cells_first, cells_second
            )
            for window_step in range(step_count)
        ]
    )
    for window_step in range(step_count):
        strain_now = forward_strain[6 * window_step : 6 * window_step + 6]
        velocity, stress, lame_accum, shear_accum = advance(
            velocity,
            stress,
            lame_first,
            shear_modulus,
            buoyancy,
            strain_now,
            surfaces[window_step],
            lame_accum,
            shear_accum,
        )
    return (velocity, stress, lame_accum, shear_accum, adjoint)


def solution(mesh):
    return jax.shard_map(
        shards,
        mesh=mesh,
        in_specs=(
            P(None, "gx", "gy", None),
            P(None, "gx", "gy", None),
            P("gx", "gy", None),
            P("gx", "gy", None),
            P("gx", "gy", None),
            P(None, "gx", "gy", None),
            P("gx", "gy", None),
            P("gx", "gy", None),
            P(("gx", "gy"), None),
            P(("gx", "gy")),
            P(),
        ),
        out_specs=(
            P(None, "gx", "gy", None),
            P(None, "gx", "gy", None),
            P("gx", "gy", None),
            P("gx", "gy", None),
            P(("gx", "gy"), None),
        ),
        check_vma=False,
    )
```

```python
import functools

import jax
import jax.numpy as jnp
from jax import lax
from jax.experimental import pallas as pl
from jax.experimental.pallas import tpu as pltpu
from jax.sharding import PartitionSpec as P

near_weight = 9.0 / 8.0
far_weight = -1.0 / 24.0
time_step = 0.25
epsilon = 1e-06


def shift_third(field, shift):
    cells = field.shape[2]
    position = lax.broadcasted_iota(jnp.int32, field.shape, 2) + shift
    moved = pltpu.roll(field, (-shift) % cells, 2)
    return jnp.where((position >= 0) & (position < cells), moved, 0.0)


def combine(at_two, at_one, at_three, at_zero):
    return near_weight * (at_two - at_one) + far_weight * (at_three - at_zero)


def third_back(field):
    return combine(field, shift_third(field, -1), shift_third(field, 1), shift_third(field, -2))


def third_ahead(field):
    return combine(shift_third(field, 1), field, shift_third(field, 2), shift_third(field, -1))


def stencil_kernel(
    counts,
    velocity,
    stress,
    lame_first,
    shear_modulus,
    buoyancy,
    strain,
    lame_accum,
    shear_accum,
    surface,
    velocity_out,
    stress_out,
    lame_out,
    shear_out,
    wide_x,
    wide_y,
    send_sem,
    recv_sem,
):
    steps = surface.shape[0]
    cells_x, cells_y = velocity.shape[1], velocity.shape[2]
    place = (lax.axis_index("gx"), lax.axis_index("gy"))

    def neighbour(axis, step):
        target = list(place)
        target[axis] = place[axis] + step
        return tuple(target)

    def present(axis, step):
        return place[axis] < counts[axis] - 1 if step > 0 else place[axis] > 0

    sides = ((0, 1), (0, -1), (1, 1), (1, -1))
    for axis, step in sides:

        @pl.when(jnp.logical_not(present(axis, step)))
        def _():
            for phase in range(2 * steps):
                if axis == 0:
                    low = cells_x + 2 if step > 0 else 0
                    wide_x[phase, :, low : low + 2] = jnp.zeros(
                        (3, 2) + velocity.shape[2:], jnp.float32
                    )
                else:
                    low = cells_y + 8 if step > 0 else 0
                    wide_y[phase, :, :, low : low + 8] = jnp.zeros(
                        (3, cells_x, 8, velocity.shape[3]), jnp.float32
                    )

    barrier = pltpu.get_barrier_semaphore()
    for axis, step in sides:

        @pl.when(present(axis, step))
        def _():
            pl.semaphore_signal(
                barrier,
                inc=1,
                device_id=neighbour(axis, step),
                device_id_type=pl.DeviceIdType.MESH,
            )

    pl.semaphore_wait(
        barrier, sum(present(axis, step).astype(jnp.int32) for axis, step in sides)
    )

    def copy_of(phase, side):
        axis, step = sides[side]
        if axis == 0:
            wide = wide_x.at[phase]
            source = wide.at[:, pl.ds(cells_x if step > 0 else 2, 2)]
            target = wide.at[:, pl.ds(0 if step > 0 else cells_x + 2, 2)]
        else:
            wide = wide_y.at[phase]
            source = wide.at[:, :, pl.ds(cells_y if step > 0 else 8, 8)]
            target = wide.at[:, :, pl.ds(0 if step > 0 else cells_y + 8, 8)]
        return pltpu.make_async_remote_copy(
            src_ref=source,
            dst_ref=target,
            send_sem=send_sem.at[phase, side],
            recv_sem=recv_sem.at[phase, side],
            device_id=neighbour(axis, step),
            device_id_type=pl.DeviceIdType.MESH,
        )

    def send(phase):
        for side, (axis, step) in enumerate(sides):

            @pl.when(present(axis, step))
            def _():
                copy_of(phase, side).start()

    def receive(phase):
        for side, (axis, step) in enumerate(sides):

            @pl.when(present(axis, -step))
            def _():
                copy_of(phase, side).wait_recv()

    def first_part(phase, part, offset):
        return wide_x[phase, part, offset : offset + cells_x]

    def second_part(phase, part, offset):
        return wide_y[phase, part, :, 6 + offset : 6 + offset + cells_y]

    def back(load, phase, part):
        return combine(*(load(phase, part, offset) for offset in (2, 1, 3, 0)))

    def ahead(load, phase, part):
        return combine(*(load(phase, part, offset) for offset in (3, 2, 4, 1)))

    def fill(phase, firsts, seconds):
        for part in range(3):
            wide_x[phase, part, 2 : 2 + cells_x] = firsts[part]
            wide_y[phase, part, :, 8 : 8 + cells_y] = seconds[part]

    for window_step in range(steps):
        held = stress if window_step == 0 else stress_out
        motion = velocity if window_step == 0 else velocity_out
        lame_from = lame_accum if window_step == 0 else lame_out
        shear_from = shear_accum if window_step == 0 else shear_out
        phase = 2 * window_step
        fill(phase, (held[0], held[3], held[4]), (held[1], held[3], held[5]))
        send(phase)
        forces = [
            third_back(held[4]),
            third_back(held[5]),
            third_ahead(held[2]) + surface[window_step],
        ]
        receive(phase)
        forces[0] += ahead(first_part, phase, 0) + back(second_part, phase, 1)
        forces[1] += back(first_part, phase, 1) + ahead(second_part, phase, 0)
        forces[2] += back(first_part, phase, 2) + back(second_part, phase, 2)
        for part in range(3):
            velocity_out[part] = motion[part] + time_step * buoyancy[...] * forces[part]
        phase += 1
        moved = [velocity_out[part] for part in range(3)]
        fill(phase, moved, moved)
        send(phase)
        rate_third = third_back(moved[2])
        shear_two = third_ahead(moved[0])
        shear_three = third_ahead(moved[1])
        receive(phase)
        rate_first = back(first_part, phase, 0)
        rate_second = back(second_part, phase, 1)
        shear_one = ahead(second_part, phase, 0) + ahead(first_part, phase, 1)
        shear_two += ahead(first_part, phase, 2)
        shear_three += ahead(second_part, phase, 2)
        dilation = rate_first + rate_second + rate_third
        spread = lame_first[...] * dilation
        stiff = shear_modulus[...]
        for part, rate in enumerate((rate_first, rate_second, rate_third)):
            stress_out[part] = held[part] + time_step * (spread + 2.0 * stiff * rate)
        for part, rate in enumerate((shear_one, shear_two, shear_three)):
            stress_out[3 + part] = held[3 + part] + time_step * (stiff * rate)
        seen = [strain[6 * window_step + part].astype(jnp.float32) for part in range(6)]
        lame_out[...] = lame_from[...] + time_step * (seen[0] + seen[1] + seen[2]) * dilation
        shear_out[...] = shear_from[...] + 2.0 * time_step * (
            seen[0] * rate_first
            + seen[1] * rate_second
            + seen[2] * rate_third
            + seen[3] * shear_one
            + seen[4] * shear_two
            + seen[5] * shear_three
        )
    for phase in range(2 * steps):
        for side, (axis, step) in enumerate(sides):

            @pl.when(present(axis, step))
            def _():
                copy_of(phase, side).wait_send()


def run_window(velocity, stress, lame_first, shear_modulus, buoyancy, strain, lame, shear, surface):
    counts = (lax.axis_size("gx"), lax.axis_size("gy"))
    steps, cells_x, cells_y, cells_z = surface.shape
    shapes = (velocity, stress, lame, shear)
    in_vmem = pl.BlockSpec(memory_space=pltpu.VMEM)
    return pl.pallas_call(
        functools.partial(stencil_kernel, counts),
        out_shape=[jax.ShapeDtypeStruct(value.shape, value.dtype) for value in shapes],
        in_specs=[in_vmem] * 9,
        out_specs=[in_vmem] * 4,
        scratch_shapes=[
            pltpu.VMEM((2 * steps, 3, cells_x + 4, cells_y, cells_z), jnp.float32),
            pltpu.VMEM((2 * steps, 3, cells_x, cells_y + 16, cells_z), jnp.float32),
            pltpu.SemaphoreType.DMA((2 * steps, 4)),
            pltpu.SemaphoreType.DMA((2 * steps, 4)),
        ],
        compiler_params=pltpu.CompilerParams(
            collective_id=0, has_side_effects=True, vmem_limit_bytes=32 * 1024 * 1024
        ),
    )(velocity, stress, lame_first, shear_modulus, buoyancy, strain, lame, shear, surface)


def split_halves(value):
    top = lax.reduce_precision(value, 8, 7)
    return top.astype(jnp.bfloat16), (value - top).astype(jnp.bfloat16)


def partner_sums(scaled, station_pairs, devices):
    stations = scaled.shape[0]
    pairs = station_pairs.shape[0]
    if stations > 1024:
        first, second = station_pairs[:, 0], station_pairs[:, 1]
        total = jnp.zeros_like(scaled).at[first].add(scaled[second])
        return total.at[second].add(scaled[first])
    held = stations // devices
    blocks = station_pairs.reshape(devices, pairs // devices, 2)
    offset = jnp.arange(devices)[:, None] * held
    first_hot = ((blocks[:, :, 0] - offset)[:, :, None] == jnp.arange(held)).astype(jnp.bfloat16)
    second_hot = (blocks[:, :, 1][:, :, None] == jnp.arange(stations)).astype(jnp.bfloat16)
    counts = (
        jnp.einsum("bpj,bpt->bjt", first_hot, second_hot, preferred_element_type=jnp.float32)
        .astype(jnp.bfloat16)
        .reshape(stations, stations)
    )
    both = jnp.concatenate(split_halves(scaled), axis=1)
    width = scaled.shape[1]
    total = lax.dot_general(
        counts, both, (((1,), (0,)), ((), ())), preferred_element_type=jnp.float32
    ) + lax.dot_general(
        counts, both, (((0,), (0,)), ((), ())), preferred_element_type=jnp.float32
    )
    return total[:, :width] + total[:, width:]


def adjoint_rows(residuals, station_pairs):
    axes = ("gx", "gy")
    held, samples = residuals.shape
    devices = lax.axis_size(axes)
    chunk = samples // devices
    values = residuals.astype(jnp.float32)
    inverse = 1.0 / jnp.sqrt(jnp.mean(values * values, axis=1, keepdims=True) + epsilon)
    inverse_top, inverse_rest = split_halves(inverse.reshape(1, held))
    scales = jnp.concatenate([inverse_top, inverse_rest], axis=0)
    scales = jnp.pad(scales, ((0, 14), (0, chunk - held)))
    payload = jnp.concatenate(
        [
            residuals.reshape(held, devices, chunk).transpose(1, 0, 2),
            jnp.broadcast_to(scales[None], (devices, 16, chunk)),
        ],
        axis=1,
    )
    arrived = lax.all_to_all(payload, axes, split_axis=0, concat_axis=0, tiled=True)
    arrived_scales = arrived[:, held, :held].astype(jnp.float32) + arrived[
        :, held + 1, :held
    ].astype(jnp.float32)
    scaled = (arrived[:, :held].astype(jnp.float32) * arrived_scales[:, :, None]).reshape(
        devices * held, chunk
    )
    sums = partner_sums(scaled, station_pairs, devices).reshape(devices, held, chunk)
    back = lax.all_to_all(sums, axes, split_axis=0, concat_axis=0, tiled=True)
    back = back.transpose(1, 0, 2).reshape(held, samples)
    normed = values * inverse
    corr_sum = jnp.mean(normed * back, axis=1, keepdims=True)
    return back - corr_sum * normed


def shards(
    velocity,
    stress,
    lame_first,
    shear_modulus,
    buoyancy,
    forward_strain,
    lame_accum,
    shear_accum,
    residuals,
    station_cell,
    station_pairs,
):
    samples = residuals.shape[1]
    adjoint = adjoint_rows(residuals, station_pairs)
    cells_first = velocity.shape[1]
    cells_second = velocity.shape[2]
    step_count = forward_strain.shape[0] // 6
    cells_hit = (station_cell[:, None] == jnp.arange(cells_first * cells_second)[None, :]).astype(
        jnp.float32
    )
    surfaces = jnp.stack(
        [
            jnp.sum(cells_hit * adjoint[:, samples - 1 - window_step][:, None], axis=0).reshape(
                cells_first, cells_second
            )
            for window_step in range(step_count)
        ]
    )
    deep = lax.broadcasted_iota(jnp.int32, surfaces.shape + (velocity.shape[3],), 3)
    surface = jnp.where(deep == 0, surfaces[..., None], 0.0)
    velocity, stress, lame_accum, shear_accum = run_window(
        velocity,
        stress,
        lame_first,
        shear_modulus,
        buoyancy,
        forward_strain,
        lame_accum,
        shear_accum,
        surface,
    )
    return (velocity, stress, lame_accum, shear_accum, adjoint)


def solution(mesh):
    return jax.shard_map(
        shards,
        mesh=mesh,
        in_specs=(
            P(None, "gx", "gy", None),
            P(None, "gx", "gy", None),
            P("gx", "gy", None),
            P("gx", "gy", None),
            P("gx", "gy", None),
            P(None, "gx", "gy", None),
            P("gx", "gy", None),
            P("gx", "gy", None),
            P(("gx", "gy"), None),
            P(("gx", "gy")),
            P(),
        ),
        out_specs=(
            P(None, "gx", "gy", None),
            P(None, "gx", "gy", None),
            P("gx", "gy", None),
            P("gx", "gy", None),
            P(("gx", "gy"), None),
        ),
        check_vma=False,
    )
```

```python
import functools

import jax
import jax.numpy as jnp
from jax import lax
from jax.experimental import pallas as pl
from jax.experimental.pallas import tpu as pltpu
from jax.sharding import PartitionSpec as P

near_weight = 9.0 / 8.0
far_weight = -1.0 / 24.0
time_step = 0.25
epsilon = 1e-06


def shift_third(field, shift):
    cells = field.shape[2]
    position = lax.broadcasted_iota(jnp.int32, field.shape, 2) + shift
    moved = pltpu.roll(field, (-shift) % cells, 2)
    return jnp.where((position >= 0) & (position < cells), moved, 0.0)


def combine(at_two, at_one, at_three, at_zero):
    return near_weight * (at_two - at_one) + far_weight * (at_three - at_zero)


def third_back(field):
    return combine(field, shift_third(field, -1), shift_third(field, 1), shift_third(field, -2))


def third_ahead(field):
    return combine(shift_third(field, 1), field, shift_third(field, 2), shift_third(field, -1))


def stencil_kernel(
    counts,
    fused,
    velocity,
    stress,
    lame_first,
    shear_modulus,
    buoyancy,
    strain,
    lame_accum,
    shear_accum,
    *rest,
):
    if fused:
        sums, residuals, inverse, hits = rest[:4]
        velocity_out, stress_out, lame_out, shear_out, adjoint = rest[4:9]
        wide_x, wide_y, send_sem, recv_sem, back_rows, fields, sum_send, sum_recv = rest[9:]
    else:
        surface, velocity_out, stress_out, lame_out, shear_out = rest[:5]
        wide_x, wide_y, send_sem, recv_sem = rest[5:]
    steps = strain.shape[0] // 6
    cells_x, cells_y = velocity.shape[1], velocity.shape[2]
    place = (lax.axis_index("gx"), lax.axis_index("gy"))

    def neighbour(axis, step):
        target = list(place)
        target[axis] = place[axis] + step
        return tuple(target)

    def present(axis, step):
        return place[axis] < counts[axis] - 1 if step > 0 else place[axis] > 0

    sides = ((0, 1), (0, -1), (1, 1), (1, -1))
    for axis, step in sides:

        @pl.when(jnp.logical_not(present(axis, step)))
        def _():
            for phase in range(2 * steps):
                if axis == 0:
                    low = cells_x + 2 if step > 0 else 0
                    wide_x[phase, :, low : low + 2] = jnp.zeros(
                        (3, 2) + velocity.shape[2:], jnp.float32
                    )
                else:
                    low = cells_y + 8 if step > 0 else 0
                    wide_y[phase, :, :, low : low + 8] = jnp.zeros(
                        (3, cells_x, 8, velocity.shape[3]), jnp.float32
                    )

    barrier = pltpu.get_barrier_semaphore()
    devices = counts[0] * counts[1]
    mine = place[0] * counts[1] + place[1]
    if fused:

        def greet(hop, carry):
            other = lax.rem(mine + hop, devices)
            pl.semaphore_signal(
                barrier,
                inc=1,
                device_id=(other // counts[1], lax.rem(other, counts[1])),
                device_id_type=pl.DeviceIdType.MESH,
            )
            return carry

        lax.fori_loop(1, devices, greet, 0)
        pl.semaphore_wait(barrier, devices - 1)
    else:
        for axis, step in sides:

            @pl.when(present(axis, step))
            def _():
                pl.semaphore_signal(
                    barrier,
                    inc=1,
                    device_id=neighbour(axis, step),
                    device_id_type=pl.DeviceIdType.MESH,
                )

        pl.semaphore_wait(
            barrier, sum(present(axis, step).astype(jnp.int32) for axis, step in sides)
        )

    def sum_copy(owner, target):
        return pltpu.make_async_remote_copy(
            src_ref=sums.at[target],
            dst_ref=back_rows.at[owner],
            send_sem=sum_send.at[target],
            recv_sem=sum_recv.at[owner],
            device_id=(target // counts[1], lax.rem(target, counts[1])),
            device_id_type=pl.DeviceIdType.MESH,
        )

    def start_sums():
        def start_one(hop, carry):
            sum_copy(mine, lax.rem(mine + hop, devices)).start()
            return carry

        lax.fori_loop(1, devices, start_one, 0)
        back_rows[pl.ds(mine, 1)] = sums[pl.ds(mine, 1)]

    def finish_sums():
        def wait_one(hop, carry):
            other = lax.rem(mine + hop, devices)
            sum_copy(other, other).wait_recv()
            return carry

        lax.fori_loop(1, devices, wait_one, 0)
        held_rows, width = back_rows.shape[1], back_rows.shape[2]
        scale = inverse[...]
        total = jnp.zeros((held_rows, width), jnp.float32)
        for part in range(devices):
            normed = residuals[:, part * width : (part + 1) * width].astype(jnp.float32) * scale
            total = total + normed * back_rows[part]
        corr_sum = jnp.sum(total, axis=1, keepdims=True) * (1.0 / (devices * width))
        for part in range(devices):
            normed = residuals[:, part * width : (part + 1) * width].astype(jnp.float32) * scale
            last = back_rows[part] - corr_sum * normed
            adjoint[:, part * width : (part + 1) * width] = last
        station = lax.broadcasted_iota(jnp.int32, last.shape, 0)
        lane = lax.broadcasted_iota(jnp.int32, last.shape, 1)
        depth = lax.broadcasted_iota(jnp.int32, hits.shape, 2)
        for window_step in range(steps):
            column = jnp.sum(
                jnp.where(lane == width - 1 - window_step, last, 0.0), axis=1, keepdims=True
            )
            row = jnp.sum(jnp.where(station == lane, column, 0.0), axis=0, keepdims=True)
            cells = jnp.sum(hits[...] * row[None], axis=2, keepdims=True)
            fields[window_step] = jnp.where(depth == 0, cells, 0.0)

    def copy_of(phase, side):
        axis, step = sides[side]
        if axis == 0:
            wide = wide_x.at[phase]
            source = wide.at[:, pl.ds(cells_x if step > 0 else 2, 2)]
            target = wide.at[:, pl.ds(0 if step > 0 else cells_x + 2, 2)]
        else:
            wide = wide_y.at[phase]
            source = wide.at[:, :, pl.ds(cells_y if step > 0 else 8, 8)]
            target = wide.at[:, :, pl.ds(0 if step > 0 else cells_y + 8, 8)]
        return pltpu.make_async_remote_copy(
            src_ref=source,
            dst_ref=target,
            send_sem=send_sem.at[phase, side],
            recv_sem=recv_sem.at[phase, side],
            device_id=neighbour(axis, step),
            device_id_type=pl.DeviceIdType.MESH,
        )

    def send(phase):
        for side, (axis, step) in enumerate(sides):

            @pl.when(present(axis, step))
            def _():
                copy_of(phase, side).start()

    def receive(phase):
        for side, (axis, step) in enumerate(sides):

            @pl.when(present(axis, -step))
            def _():
                copy_of(phase, side).wait_recv()

    def first_part(phase, part, offset):
        return wide_x[phase, part, offset : offset + cells_x]

    def second_part(phase, part, offset):
        return wide_y[phase, part, :, 6 + offset : 6 + offset + cells_y]

    def back(load, phase, part):
        return combine(*(load(phase, part, offset) for offset in (2, 1, 3, 0)))

    def ahead(load, phase, part):
        return combine(*(load(phase, part, offset) for offset in (3, 2, 4, 1)))

    def fill(phase, firsts, seconds):
        for part in range(3):
            wide_x[phase, part, 2 : 2 + cells_x] = firsts[part]
            wide_y[phase, part, :, 8 : 8 + cells_y] = seconds[part]

    for window_step in range(steps):
        held = stress if window_step == 0 else stress_out
        motion = velocity if window_step == 0 else velocity_out
        lame_from = lame_accum if window_step == 0 else lame_out
        shear_from = shear_accum if window_step == 0 else shear_out
        phase = 2 * window_step
        fill(phase, (held[0], held[3], held[4]), (held[1], held[3], held[5]))
        send(phase)
        if fused and window_step == 0:
            start_sums()
        forces = [third_back(held[4]), third_back(held[5]), third_ahead(held[2])]
        if not fused:
            forces[2] += surface[window_step]
        elif window_step > 0:
            forces[2] += fields[window_step]
        receive(phase)
        forces[0] += ahead(first_part, phase, 0) + back(second_part, phase, 1)
        forces[1] += back(first_part, phase, 1) + ahead(second_part, phase, 0)
        forces[2] += back(first_part, phase, 2) + back(second_part, phase, 2)
        for part in range(3):
            velocity_out[part] = motion[part] + time_step * buoyancy[...] * forces[part]
        if fused and window_step == 0:
            finish_sums()
            velocity_out[2] += time_step * buoyancy[...] * fields[0]
        phase += 1
        moved = [velocity_out[part] for part in range(3)]
        fill(phase, moved, moved)
        send(phase)
        rate_third = third_back(moved[2])
        shear_two = third_ahead(moved[0])
        shear_three = third_ahead(moved[1])
        receive(phase)
        rate_first = back(first_part, phase, 0)
        rate_second = back(second_part, phase, 1)
        shear_one = ahead(second_part, phase, 0) + ahead(first_part, phase, 1)
        shear_two += ahead(first_part, phase, 2)
        shear_three += ahead(second_part, phase, 2)
        dilation = rate_first + rate_second + rate_third
        spread = lame_first[...] * dilation
        stiff = shear_modulus[...]
        for part, rate in enumerate((rate_first, rate_second, rate_third)):
            stress_out[part] = held[part] + time_step * (spread + 2.0 * stiff * rate)
        for part, rate in enumerate((shear_one, shear_two, shear_three)):
            stress_out[3 + part] = held[3 + part] + time_step * (stiff * rate)
        seen = [strain[6 * window_step + part].astype(jnp.float32) for part in range(6)]
        lame_out[...] = lame_from[...] + time_step * (seen[0] + seen[1] + seen[2]) * dilation
        shear_out[...] = shear_from[...] + 2.0 * time_step * (
            seen[0] * rate_first
            + seen[1] * rate_second
            + seen[2] * rate_third
            + seen[3] * shear_one
            + seen[4] * shear_two
            + seen[5] * shear_three
        )
    for phase in range(2 * steps):
        for side, (axis, step) in enumerate(sides):

            @pl.when(present(axis, step))
            def _():
                copy_of(phase, side).wait_send()

    if fused:

        def wait_sent(hop, carry):
            other = lax.rem(mine + hop, devices)
            sum_copy(mine, other).wait_send()
            return carry

        lax.fori_loop(1, devices, wait_sent, 0)


def run_window(velocity, stress, lame_first, shear_modulus, buoyancy, strain, lame, shear, extra):
    counts = (lax.axis_size("gx"), lax.axis_size("gy"))
    devices = counts[0] * counts[1]
    fused = len(extra) > 1
    cells_x, cells_y, cells_z = velocity.shape[1:]
    steps = strain.shape[0] // 6
    shapes = [
        jax.ShapeDtypeStruct(value.shape, value.dtype) for value in (velocity, stress, lame, shear)
    ]
    scratch = [
        pltpu.VMEM((2 * steps, 3, cells_x + 4, cells_y, cells_z), jnp.float32),
        pltpu.VMEM((2 * steps, 3, cells_x, cells_y + 16, cells_z), jnp.float32),
        pltpu.SemaphoreType.DMA((2 * steps, 4)),
        pltpu.SemaphoreType.DMA((2 * steps, 4)),
    ]
    if fused:
        shapes.append(jax.ShapeDtypeStruct(extra[1].shape, jnp.float32))
        scratch += [
            pltpu.VMEM(extra[0].shape, jnp.float32),
            pltpu.VMEM((steps, cells_x, cells_y, cells_z), jnp.float32),
            pltpu.SemaphoreType.DMA((devices,)),
            pltpu.SemaphoreType.DMA((devices,)),
        ]
    in_vmem = pl.BlockSpec(memory_space=pltpu.VMEM)
    return pl.pallas_call(
        functools.partial(stencil_kernel, counts, fused),
        out_shape=shapes,
        in_specs=[in_vmem] * (8 + len(extra)),
        out_specs=[in_vmem] * len(shapes),
        scratch_shapes=scratch,
        compiler_params=pltpu.CompilerParams(
            collective_id=0, has_side_effects=True, vmem_limit_bytes=32 * 1024 * 1024
        ),
    )(velocity, stress, lame_first, shear_modulus, buoyancy, strain, lame, shear, *extra)


def split_halves(value):
    top = lax.reduce_precision(value, 8, 7)
    return top.astype(jnp.bfloat16), (value - top).astype(jnp.bfloat16)


def partner_sums(scaled, station_pairs, devices):
    stations = scaled.shape[0]
    pairs = station_pairs.shape[0]
    if stations > 1024:
        first, second = station_pairs[:, 0], station_pairs[:, 1]
        total = jnp.zeros_like(scaled).at[first].add(scaled[second])
        return total.at[second].add(scaled[first])
    held = stations // devices
    blocks = station_pairs.reshape(devices, pairs // devices, 2)
    offset = jnp.arange(devices)[:, None] * held
    first_hot = ((blocks[:, :, 0] - offset)[:, :, None] == jnp.arange(held)).astype(jnp.bfloat16)
    second_hot = (blocks[:, :, 1][:, :, None] == jnp.arange(stations)).astype(jnp.bfloat16)
    counts = (
        jnp.einsum("bpj,bpt->bjt", first_hot, second_hot, preferred_element_type=jnp.float32)
        .astype(jnp.bfloat16)
        .reshape(stations, stations)
    )
    both = jnp.concatenate(split_halves(scaled), axis=1)
    width = scaled.shape[1]
    total = lax.dot_general(
        counts, both, (((1,), (0,)), ((), ())), preferred_element_type=jnp.float32
    ) + lax.dot_general(
        counts, both, (((0,), (0,)), ((), ())), preferred_element_type=jnp.float32
    )
    return total[:, :width] + total[:, width:]


def shard_sums(residuals, station_pairs):
    axes = ("gx", "gy")
    held, samples = residuals.shape
    devices = lax.axis_size(axes)
    chunk = samples // devices
    values = residuals.astype(jnp.float32)
    inverse = 1.0 / jnp.sqrt(jnp.mean(values * values, axis=1, keepdims=True) + epsilon)
    inverse_top, inverse_rest = split_halves(inverse.reshape(1, held))
    scales = jnp.concatenate([inverse_top, inverse_rest], axis=0)
    scales = jnp.pad(scales, ((0, 14), (0, chunk - held)))
    payload = jnp.concatenate(
        [
            residuals.reshape(held, devices, chunk).transpose(1, 0, 2),
            jnp.broadcast_to(scales[None], (devices, 16, chunk)),
        ],
        axis=1,
    )
    arrived = lax.all_to_all(payload, axes, split_axis=0, concat_axis=0, tiled=True)
    arrived_scales = arrived[:, held, :held].astype(jnp.float32) + arrived[
        :, held + 1, :held
    ].astype(jnp.float32)
    scaled = (arrived[:, :held].astype(jnp.float32) * arrived_scales[:, :, None]).reshape(
        devices * held, chunk
    )
    sums = partner_sums(scaled, station_pairs, devices).reshape(devices, held, chunk)
    return sums, inverse


def adjoint_rows(sums, residuals, inverse):
    axes = ("gx", "gy")
    held, samples = residuals.shape
    values = residuals.astype(jnp.float32)
    back = lax.all_to_all(sums, axes, split_axis=0, concat_axis=0, tiled=True)
    back = back.transpose(1, 0, 2).reshape(held, samples)
    normed = values * inverse
    corr_sum = jnp.mean(normed * back, axis=1, keepdims=True)
    return back - corr_sum * normed


def shards(
    velocity,
    stress,
    lame_first,
    shear_modulus,
    buoyancy,
    forward_strain,
    lame_accum,
    shear_accum,
    residuals,
    station_cell,
    station_pairs,
):
    samples = residuals.shape[1]
    sums, inverse = shard_sums(residuals, station_pairs)
    fields = (
        velocity,
        stress,
        lame_first,
        shear_modulus,
        buoyancy,
        forward_strain,
        lame_accum,
        shear_accum,
    )
    if sums.shape[2] % 128 == 0 and sums.shape[2] == velocity.shape[3]:
        cells = velocity.shape[1] * velocity.shape[2]
        stations = jnp.pad(station_cell, (0, sums.shape[2] - sums.shape[1]), constant_values=-1)
        hits = (jnp.arange(cells)[:, None] == stations[None, :]).astype(jnp.float32)
        hits = hits.reshape(velocity.shape[1:3] + (sums.shape[2],))
        return tuple(run_window(*fields, (sums, residuals, inverse, hits)))
    adjoint = adjoint_rows(sums, residuals, inverse)
    cells_first = velocity.shape[1]
    cells_second = velocity.shape[2]
    step_count = forward_strain.shape[0] // 6
    cells_hit = (station_cell[:, None] == jnp.arange(cells_first * cells_second)[None, :]).astype(
        jnp.float32
    )
    surfaces = jnp.stack(
        [
            jnp.sum(cells_hit * adjoint[:, samples - 1 - window_step][:, None], axis=0).reshape(
                cells_first, cells_second
            )
            for window_step in range(step_count)
        ]
    )
    deep = lax.broadcasted_iota(jnp.int32, surfaces.shape + (velocity.shape[3],), 3)
    surface = jnp.where(deep == 0, surfaces[..., None], 0.0)
    return (*run_window(*fields, (surface,)), adjoint)


def solution(mesh):
    return jax.shard_map(
        shards,
        mesh=mesh,
        in_specs=(
            P(None, "gx", "gy", None),
            P(None, "gx", "gy", None),
            P("gx", "gy", None),
            P("gx", "gy", None),
            P("gx", "gy", None),
            P(None, "gx", "gy", None),
            P("gx", "gy", None),
            P("gx", "gy", None),
            P(("gx", "gy"), None),
            P(("gx", "gy")),
            P(),
        ),
        out_specs=(
            P(None, "gx", "gy", None),
            P(None, "gx", "gy", None),
            P("gx", "gy", None),
            P("gx", "gy", None),
            P(("gx", "gy"), None),
        ),
        check_vma=False,
    )
```

```python
import functools

import jax
import jax.numpy as jnp
from jax import lax
from jax.experimental import pallas as pl
from jax.experimental.pallas import tpu as pltpu
from jax.sharding import PartitionSpec as P

near_weight = 9.0 / 8.0
far_weight = -1.0 / 24.0
time_step = 0.25
epsilon = 1e-06


def shift_third(field, shift):
    cells = field.shape[2]
    position = lax.broadcasted_iota(jnp.int32, field.shape, 2) + shift
    moved = pltpu.roll(field, (-shift) % cells, 2)
    return jnp.where((position >= 0) & (position < cells), moved, 0.0)


def combine(at_two, at_one, at_three, at_zero):
    return near_weight * (at_two - at_one) + far_weight * (at_three - at_zero)


def third_back(field):
    return combine(field, shift_third(field, -1), shift_third(field, 1), shift_third(field, -2))


def third_ahead(field):
    return combine(shift_third(field, 1), field, shift_third(field, 2), shift_third(field, -1))


def stencil_kernel(
    counts,
    fused,
    velocity,
    stress,
    lame_first,
    shear_modulus,
    buoyancy,
    strain,
    lame_accum,
    shear_accum,
    *rest,
):
    if fused:
        sums, residuals, inverse, hits = rest[:4]
        velocity_out, stress_out, lame_out, shear_out, adjoint = rest[4:9]
        wide_x, wide_y, send_sem, recv_sem, back_rows, fields, sum_send, sum_recv = rest[9:]
    else:
        surface, velocity_out, stress_out, lame_out, shear_out = rest[:5]
        wide_x, wide_y, send_sem, recv_sem = rest[5:]
    steps = strain.shape[0] // 6
    cells_x, cells_y = velocity.shape[1], velocity.shape[2]
    place = (lax.axis_index("gx"), lax.axis_index("gy"))

    def neighbour(axis, step):
        target = list(place)
        target[axis] = place[axis] + step
        return tuple(target)

    def present(axis, step):
        return place[axis] < counts[axis] - 1 if step > 0 else place[axis] > 0

    sides = ((0, 1), (0, -1), (1, 1), (1, -1))
    for axis, step in sides:

        @pl.when(jnp.logical_not(present(axis, step)))
        def _():
            for phase in range(2 * steps):
                if axis == 0:
                    low = cells_x + 2 if step > 0 else 0
                    wide_x[phase, :, low : low + 2] = jnp.zeros(
                        (3, 2) + velocity.shape[2:], jnp.float32
                    )
                else:
                    low = cells_y + 8 if step > 0 else 0
                    wide_y[phase, :, :, low : low + 8] = jnp.zeros(
                        (3, cells_x, 8, velocity.shape[3]), jnp.float32
                    )

    barrier = pltpu.get_barrier_semaphore()
    devices = counts[0] * counts[1]
    mine = place[0] * counts[1] + place[1]
    if fused:

        def greet(hop, carry):
            other = lax.rem(mine + hop, devices)
            pl.semaphore_signal(
                barrier,
                inc=1,
                device_id=(other // counts[1], lax.rem(other, counts[1])),
                device_id_type=pl.DeviceIdType.MESH,
            )
            return carry

        lax.fori_loop(1, devices, greet, 0)
        pl.semaphore_wait(barrier, devices - 1)
    else:
        for axis, step in sides:

            @pl.when(present(axis, step))
            def _():
                pl.semaphore_signal(
                    barrier,
                    inc=1,
                    device_id=neighbour(axis, step),
                    device_id_type=pl.DeviceIdType.MESH,
                )

        pl.semaphore_wait(
            barrier, sum(present(axis, step).astype(jnp.int32) for axis, step in sides)
        )

    def sum_copy(owner, target):
        return pltpu.make_async_remote_copy(
            src_ref=sums.at[target],
            dst_ref=back_rows.at[owner],
            send_sem=sum_send.at[target],
            recv_sem=sum_recv.at[owner],
            device_id=(target // counts[1], lax.rem(target, counts[1])),
            device_id_type=pl.DeviceIdType.MESH,
        )

    def start_sums():
        def start_one(hop, carry):
            sum_copy(mine, lax.rem(mine + hop, devices)).start()
            return carry

        lax.fori_loop(1, devices, start_one, 0)
        back_rows[pl.ds(mine, 1)] = sums[pl.ds(mine, 1)]

    def finish_sums():
        def wait_one(hop, carry):
            other = lax.rem(mine + hop, devices)
            sum_copy(other, other).wait_recv()
            return carry

        lax.fori_loop(1, devices, wait_one, 0)
        held_rows, width = back_rows.shape[1], back_rows.shape[2]
        scale = inverse[...]
        total = jnp.zeros((held_rows, width), jnp.float32)
        for part in range(devices):
            normed = residuals[:, part * width : (part + 1) * width].astype(jnp.float32) * scale
            total = total + normed * back_rows[part]
        corr_sum = jnp.sum(total, axis=1, keepdims=True) * (1.0 / (devices * width))
        last = back_rows[devices - 1] - corr_sum * normed
        station = lax.broadcasted_iota(jnp.int32, last.shape, 0)
        lane = lax.broadcasted_iota(jnp.int32, last.shape, 1)
        depth = lax.broadcasted_iota(jnp.int32, hits.shape, 2)
        for window_step in range(steps):
            column = jnp.sum(
                jnp.where(lane == width - 1 - window_step, last, 0.0), axis=1, keepdims=True
            )
            row = jnp.sum(jnp.where(station == lane, column, 0.0), axis=0, keepdims=True)
            cells = jnp.sum(hits[...] * row[None], axis=2, keepdims=True)
            fields[window_step] = jnp.where(depth == 0, cells, 0.0)
        return corr_sum * scale

    def write_adjoint(own_weight):
        width = back_rows.shape[2]
        for part in range(devices):
            own = residuals[:, part * width : (part + 1) * width].astype(jnp.float32)
            adjoint[:, part * width : (part + 1) * width] = back_rows[part] - own_weight * own

    def copy_of(phase, side):
        axis, step = sides[side]
        if axis == 0:
            wide = wide_x.at[phase]
            source = wide.at[:, pl.ds(cells_x if step > 0 else 2, 2)]
            target = wide.at[:, pl.ds(0 if step > 0 else cells_x + 2, 2)]
        else:
            wide = wide_y.at[phase]
            source = wide.at[:, :, pl.ds(cells_y if step > 0 else 8, 8)]
            target = wide.at[:, :, pl.ds(0 if step > 0 else cells_y + 8, 8)]
        return pltpu.make_async_remote_copy(
            src_ref=source,
            dst_ref=target,
            send_sem=send_sem.at[phase, side],
            recv_sem=recv_sem.at[phase, side],
            device_id=neighbour(axis, step),
            device_id_type=pl.DeviceIdType.MESH,
        )

    def send(phase):
        for side, (axis, step) in enumerate(sides):

            @pl.when(present(axis, step))
            def _():
                copy_of(phase, side).start()

    def receive(phase):
        for side, (axis, step) in enumerate(sides):

            @pl.when(present(axis, -step))
            def _():
                copy_of(phase, side).wait_recv()

    def first_part(phase, part, offset):
        return wide_x[phase, part, offset : offset + cells_x]

    def second_part(phase, part, offset):
        return wide_y[phase, part, :, 6 + offset : 6 + offset + cells_y]

    def back(load, phase, part):
        return combine(*(load(phase, part, offset) for offset in (2, 1, 3, 0)))

    def ahead(load, phase, part):
        return combine(*(load(phase, part, offset) for offset in (3, 2, 4, 1)))

    def fill(phase, firsts, seconds):
        for part in range(3):
            wide_x[phase, part, 2 : 2 + cells_x] = firsts[part]
            wide_y[phase, part, :, 8 : 8 + cells_y] = seconds[part]

    for window_step in range(steps):
        held = stress if window_step == 0 else stress_out
        motion = velocity if window_step == 0 else velocity_out
        lame_from = lame_accum if window_step == 0 else lame_out
        shear_from = shear_accum if window_step == 0 else shear_out
        phase = 2 * window_step
        fill(phase, (held[0], held[3], held[4]), (held[1], held[3], held[5]))
        send(phase)
        if fused and window_step == 0:
            start_sums()
        forces = [third_back(held[4]), third_back(held[5]), third_ahead(held[2])]
        if not fused:
            forces[2] += surface[window_step]
        elif window_step > 0:
            forces[2] += fields[window_step]
        receive(phase)
        forces[0] += ahead(first_part, phase, 0) + back(second_part, phase, 1)
        forces[1] += back(first_part, phase, 1) + ahead(second_part, phase, 0)
        forces[2] += back(first_part, phase, 2) + back(second_part, phase, 2)
        for part in range(3):
            velocity_out[part] = motion[part] + time_step * buoyancy[...] * forces[part]
        if fused and window_step == 0:
            own_weight = finish_sums()
            velocity_out[2] += time_step * buoyancy[...] * fields[0]
        phase += 1
        moved = [velocity_out[part] for part in range(3)]
        fill(phase, moved, moved)
        send(phase)
        if fused and window_step == 0:
            write_adjoint(own_weight)
        rate_third = third_back(moved[2])
        shear_two = third_ahead(moved[0])
        shear_three = third_ahead(moved[1])
        receive(phase)
        rate_first = back(first_part, phase, 0)
        rate_second = back(second_part, phase, 1)
        shear_one = ahead(second_part, phase, 0) + ahead(first_part, phase, 1)
        shear_two += ahead(first_part, phase, 2)
        shear_three += ahead(second_part, phase, 2)
        dilation = rate_first + rate_second + rate_third
        spread = lame_first[...] * dilation
        stiff = shear_modulus[...]
        for part, rate in enumerate((rate_first, rate_second, rate_third)):
            stress_out[part] = held[part] + time_step * (spread + 2.0 * stiff * rate)
        for part, rate in enumerate((shear_one, shear_two, shear_three)):
            stress_out[3 + part] = held[3 + part] + time_step * (stiff * rate)
        seen = [strain[6 * window_step + part].astype(jnp.float32) for part in range(6)]
        lame_out[...] = lame_from[...] + time_step * (seen[0] + seen[1] + seen[2]) * dilation
        shear_out[...] = shear_from[...] + 2.0 * time_step * (
            seen[0] * rate_first
            + seen[1] * rate_second
            + seen[2] * rate_third
            + seen[3] * shear_one
            + seen[4] * shear_two
            + seen[5] * shear_three
        )
    for phase in range(2 * steps):
        for side, (axis, step) in enumerate(sides):

            @pl.when(present(axis, step))
            def _():
                copy_of(phase, side).wait_send()

    if fused:

        def wait_sent(hop, carry):
            other = lax.rem(mine + hop, devices)
            sum_copy(mine, other).wait_send()
            return carry

        lax.fori_loop(1, devices, wait_sent, 0)


def run_window(velocity, stress, lame_first, shear_modulus, buoyancy, strain, lame, shear, extra):
    counts = (lax.axis_size("gx"), lax.axis_size("gy"))
    devices = counts[0] * counts[1]
    fused = len(extra) > 1
    cells_x, cells_y, cells_z = velocity.shape[1:]
    steps = strain.shape[0] // 6
    shapes = [
        jax.ShapeDtypeStruct(value.shape, value.dtype) for value in (velocity, stress, lame, shear)
    ]
    scratch = [
        pltpu.VMEM((2 * steps, 3, cells_x + 4, cells_y, cells_z), jnp.float32),
        pltpu.VMEM((2 * steps, 3, cells_x, cells_y + 16, cells_z), jnp.float32),
        pltpu.SemaphoreType.DMA((2 * steps, 4)),
        pltpu.SemaphoreType.DMA((2 * steps, 4)),
    ]
    if fused:
        shapes.append(jax.ShapeDtypeStruct(extra[1].shape, jnp.float32))
        scratch += [
            pltpu.VMEM(extra[0].shape, jnp.float32),
            pltpu.VMEM((steps, cells_x, cells_y, cells_z), jnp.float32),
            pltpu.SemaphoreType.DMA((devices,)),
            pltpu.SemaphoreType.DMA((devices,)),
        ]
    in_vmem = pl.BlockSpec(memory_space=pltpu.VMEM)
    return pl.pallas_call(
        functools.partial(stencil_kernel, counts, fused),
        out_shape=shapes,
        in_specs=[in_vmem] * (8 + len(extra)),
        out_specs=[in_vmem] * len(shapes),
        scratch_shapes=scratch,
        compiler_params=pltpu.CompilerParams(
            collective_id=0, has_side_effects=True, vmem_limit_bytes=32 * 1024 * 1024
        ),
    )(velocity, stress, lame_first, shear_modulus, buoyancy, strain, lame, shear, *extra)


def split_halves(value):
    top = lax.reduce_precision(value, 8, 7)
    return top.astype(jnp.bfloat16), (value - top).astype(jnp.bfloat16)


def partner_sums(scaled, station_pairs, devices):
    stations = scaled.shape[0]
    pairs = station_pairs.shape[0]
    if stations > 1024:
        first, second = station_pairs[:, 0], station_pairs[:, 1]
        total = jnp.zeros_like(scaled).at[first].add(scaled[second])
        return total.at[second].add(scaled[first])
    held = stations // devices
    blocks = station_pairs.reshape(devices, pairs // devices, 2)
    offset = jnp.arange(devices)[:, None] * held
    first_hot = ((blocks[:, :, 0] - offset)[:, :, None] == jnp.arange(held)).astype(jnp.bfloat16)
    second_hot = (blocks[:, :, 1][:, :, None] == jnp.arange(stations)).astype(jnp.bfloat16)
    counts = (
        jnp.einsum("bpj,bpt->bjt", first_hot, second_hot, preferred_element_type=jnp.float32)
        .astype(jnp.bfloat16)
        .reshape(stations, stations)
    )
    both = jnp.concatenate(split_halves(scaled), axis=1)
    width = scaled.shape[1]
    total = lax.dot_general(
        counts, both, (((1,), (0,)), ((), ())), preferred_element_type=jnp.float32
    ) + lax.dot_general(
        counts, both, (((0,), (0,)), ((), ())), preferred_element_type=jnp.float32
    )
    return total[:, :width] + total[:, width:]


def shard_sums(residuals, station_pairs):
    axes = ("gx", "gy")
    held, samples = residuals.shape
    devices = lax.axis_size(axes)
    chunk = samples // devices
    values = residuals.astype(jnp.float32)
    inverse = 1.0 / jnp.sqrt(jnp.mean(values * values, axis=1, keepdims=True) + epsilon)
    inverse_top, inverse_rest = split_halves(inverse.reshape(1, held))
    scales = jnp.concatenate([inverse_top, inverse_rest], axis=0)
    scales = jnp.pad(scales, ((0, 14), (0, chunk - held)))
    payload = jnp.concatenate(
        [
            residuals.reshape(held, devices, chunk).transpose(1, 0, 2),
            jnp.broadcast_to(scales[None], (devices, 16, chunk)),
        ],
        axis=1,
    )
    arrived = lax.all_to_all(payload, axes, split_axis=0, concat_axis=0, tiled=True)
    arrived_scales = arrived[:, held, :held].astype(jnp.float32) + arrived[
        :, held + 1, :held
    ].astype(jnp.float32)
    scaled = (arrived[:, :held].astype(jnp.float32) * arrived_scales[:, :, None]).reshape(
        devices * held, chunk
    )
    sums = partner_sums(scaled, station_pairs, devices).reshape(devices, held, chunk)
    return sums, inverse


def adjoint_rows(sums, residuals, inverse):
    axes = ("gx", "gy")
    held, samples = residuals.shape
    values = residuals.astype(jnp.float32)
    back = lax.all_to_all(sums, axes, split_axis=0, concat_axis=0, tiled=True)
    back = back.transpose(1, 0, 2).reshape(held, samples)
    normed = values * inverse
    corr_sum = jnp.mean(normed * back, axis=1, keepdims=True)
    return back - corr_sum * normed


def shards(
    velocity,
    stress,
    lame_first,
    shear_modulus,
    buoyancy,
    forward_strain,
    lame_accum,
    shear_accum,
    residuals,
    station_cell,
    station_pairs,
):
    samples = residuals.shape[1]
    sums, inverse = shard_sums(residuals, station_pairs)
    fields = (
        velocity,
        stress,
        lame_first,
        shear_modulus,
        buoyancy,
        forward_strain,
        lame_accum,
        shear_accum,
    )
    if sums.shape[2] % 128 == 0 and sums.shape[2] == velocity.shape[3]:
        cells = velocity.shape[1] * velocity.shape[2]
        stations = jnp.pad(station_cell, (0, sums.shape[2] - sums.shape[1]), constant_values=-1)
        hits = (jnp.arange(cells)[:, None] == stations[None, :]).astype(jnp.float32)
        hits = hits.reshape(velocity.shape[1:3] + (sums.shape[2],))
        return tuple(run_window(*fields, (sums, residuals, inverse, hits)))
    adjoint = adjoint_rows(sums, residuals, inverse)
    cells_first = velocity.shape[1]
    cells_second = velocity.shape[2]
    step_count = forward_strain.shape[0] // 6
    cells_hit = (station_cell[:, None] == jnp.arange(cells_first * cells_second)[None, :]).astype(
        jnp.float32
    )
    surfaces = jnp.stack(
        [
            jnp.sum(cells_hit * adjoint[:, samples - 1 - window_step][:, None], axis=0).reshape(
                cells_first, cells_second
            )
            for window_step in range(step_count)
        ]
    )
    deep = lax.broadcasted_iota(jnp.int32, surfaces.shape + (velocity.shape[3],), 3)
    surface = jnp.where(deep == 0, surfaces[..., None], 0.0)
    return (*run_window(*fields, (surface,)), adjoint)


def solution(mesh):
    return jax.shard_map(
        shards,
        mesh=mesh,
        in_specs=(
            P(None, "gx", "gy", None),
            P(None, "gx", "gy", None),
            P("gx", "gy", None),
            P("gx", "gy", None),
            P("gx", "gy", None),
            P(None, "gx", "gy", None),
            P("gx", "gy", None),
            P("gx", "gy", None),
            P(("gx", "gy"), None),
            P(("gx", "gy")),
            P(),
        ),
        out_specs=(
            P(None, "gx", "gy", None),
            P(None, "gx", "gy", None),
            P("gx", "gy", None),
            P("gx", "gy", None),
            P(("gx", "gy"), None),
        ),
        check_vma=False,
    )
```
